32 devices in a mesh: aux: 4 (over x, core), pair: 8 (over z, y).
Axes of the slice: x: 2, y: 2, z: 4, core: 2. Of those that a mesh axis runs over, the one named last changes fastest.
Arguments:
- three_centre: bfloat16 [48, 32, 128, 128], P('aux', 'pair'), may hold values from -6 to 6
- occ_green: bfloat16 [1024, 1024], P('pair'), as said below
- virt_green: bfloat16 [1024, 1024], replicated, may hold values from -0.25 to 0.25
- tile_cols: int32 [8, 4], replicated, may hold values from 0 to 7, as said below
- tile_live: int32 [8], replicated, may hold values from 1 to 4, as said below
Outputs:
- polarizability: float32 [48, 48], P('pair', 'aux')
The draws below stay inside these ranges and needn't reach their ends.
Inputs may be any that keep to these rules, and one draw needn't show every extreme that they name: occ_green is symmetric. `tile_cols`: the 4 column blocks of one block row are distinct. `tile_live`: some block row has all 4 slots live.
All inputs are finite; a program needn't handle non-finite values.
Results may differ from the reference program's by a relative error of at most 0.015.
Values may be sent and summed in bfloat16 or wider, within the bound.
No kernel may reach another device: no remote copies, remote signals or barrier semaphores. Data moves between devices by JAX's collectives and lax.ppermute only.
A program may use at most 192 MiB of HBM per device.

```python
import math
import jax
import jax.numpy as jnp
from jax import lax

TB = 128
TILE = 4
NBLK = 8
NB = 1024
NT = 32
NAUX = 48
N_PAIR = 8


def draw_occ_green(key, part):
    base = jax.random.normal(key, (NB, NB), jnp.float32)
    return ((base + base.T) * (0.5 / NB) ** 0.5).astype(jnp.bfloat16)


def draw_tile_cols(key, part):
    row_keys = jax.random.split(key, NBLK)
    picked = jax.vmap(lambda single: jax.random.permutation(single, NBLK)[:TILE])(row_keys)
    return picked.astype(jnp.int32)


def draw_tile_live(key, part):
    counts = jax.random.randint(key, (NBLK,), 1, TILE + 1)
    fullest = jax.random.randint(jax.random.fold_in(key, 3), (), 0, NBLK)
    return jnp.where(jnp.arange(NBLK) == fullest, TILE, counts).astype(jnp.int32)


def block_scale(key, extent, shards, least, top_value):
    def one(position, blocks):
        heights = jax.random.uniform(jax.random.fold_in(jax.random.fold_in(key, 6), position), (blocks,), jnp.float32, least / len(shards), top_value / len(shards))
        return jnp.repeat(jnp.exp(heights), extent[position] // blocks).reshape((-1,) + (1,) * (len(extent) - position - 1))

    level = one(*shards[0])
    for cut in shards[1:]:
        level = level * one(*cut)
    return level


def noise(stream_key, shape, width, limit, shards=(), kind=jnp.bfloat16):
    level = block_scale(stream_key, shape, shards, -0.22, 0.18) if shards else 1.0
    values = jax.random.normal(stream_key, shape, jnp.float32) * width * level
    return jnp.minimum(jnp.maximum(values, -limit), limit).astype(kind)


def setup_inputs(seed: int = 0) -> dict:
    seeds = jax.random.split(jax.random.key(seed), 6)
    three_centre = noise(seeds[0], (NAUX, NT, TB, TB), 1.0, 6.0, ((0, 4), (1, 8)))
    occ_green = draw_occ_green(jax.random.fold_in(seeds[5], 71), 0)
    virt_green = noise(seeds[2], (NB, NB), (TB * TILE) ** -0.5, 0.25)
    tile_cols = draw_tile_cols(jax.random.fold_in(seeds[5], 71), 0)
    tile_live = draw_tile_live(jax.random.fold_in(seeds[5], 71), 0)
    return {"three_centre": three_centre, "occ_green": occ_green, "virt_green": virt_green, "tile_cols": tile_cols, "tile_live": tile_live}


def reference(three_centre, occ_green, virt_green, tile_cols, tile_live):
    slot_index = jnp.arange(TILE, dtype=jnp.int32)
    live_rows = (slot_index[None, :] < tile_live[:, None]).astype(jnp.float32)
    flat_cols = tile_cols.reshape(NT).astype(jnp.int32)
    virt_rows = jnp.take(virt_green.reshape(N_PAIR, TB, NB), flat_cols, axis=0)
    virt_rows = virt_rows.astype(jnp.float32).reshape(N_PAIR, TILE, TB, N_PAIR, TB)
    occ_blocks = occ_green.astype(jnp.float32).reshape(N_PAIR, TB, N_PAIR, TB)

    def one_row(tiles):
        blocks = tiles.astype(jnp.float32).reshape(N_PAIR, TILE, TB, TB) * live_rows[:, :, None, None]
        half = jnp.einsum('ksab,ksbjc->kajc', blocks, virt_rows)
        half = lax.optimization_barrier(half.astype(jnp.bfloat16)).astype(jnp.float32)
        picked = jnp.take(half, flat_cols, axis=2)
        picked = picked.reshape(N_PAIR, TB, N_PAIR, TILE, TB)
        terms = jnp.einsum('iakb,kbisc->kisac', occ_blocks, picked)
        terms = lax.optimization_barrier(terms.astype(jnp.bfloat16)).astype(jnp.float32)
        polar = lax.optimization_barrier(jnp.sum(terms, axis=0))
        return polar.astype(jnp.bfloat16).reshape(NT * TB * TB)
    polar_tiles = lax.map(one_row, three_centre)
    live_flat = live_rows.reshape(NT).astype(jnp.bfloat16)
    masked = (three_centre * live_flat[None, :, None, None]).reshape(NAUX, NT * TB * TB)
    chi = lax.dot_general(masked, polar_tiles, (((1,), (1,)), ((), ())), preferred_element_type=jnp.float32)
    return chi * (1.0 / (TB * math.sqrt(NT)))
```

```python
import math

import jax
import jax.numpy as jnp
from jax import lax
from jax.experimental import pallas as pl
from jax.experimental.pallas import tpu as pltpu
from jax.sharding import PartitionSpec as P

F32 = jnp.float32
BF16 = jnp.bfloat16
VMEM = pl.BlockSpec(memory_space=pltpu.VMEM)
SMEM = pl.BlockSpec(memory_space=pltpu.SMEM)


def split_kernel(groups, lows, tiles_ref, *outs):
    high = lax.axis_index("pair") // lows
    for n, out in enumerate(outs):
        c, d = divmod(n, groups)
        out[...] = tiles_ref[c * groups + lax.rem(high + d, groups)]


def split(tiles, groups, lows):
    count = tiles.shape[0]
    piece = jax.ShapeDtypeStruct(tiles.shape[1:], tiles.dtype)
    return pl.pallas_call(
        lambda *refs: split_kernel(groups, lows, *refs),
        out_shape=[piece] * count,
        in_specs=[VMEM],
        out_specs=[VMEM] * count,
        name="split",
    )(tiles)


def polar_kernel(groups, lows, cols_ref, live_ref, virt_ref, *rest):
    own = rest[:groups]
    others = rest[groups : groups + lows - 1]
    occ = rest[groups + lows - 1 : 2 * groups + lows - 1]
    outs = rest[2 * groups + lows - 1 : 3 * groups + lows - 1]
    half, lhs, full = rest[3 * groups + lows - 1 :]
    slots, width = own[0].shape[0], own[0].shape[1]
    basis = virt_ref.shape[0]
    me = lax.axis_index("pair")
    high, low = me // lows, lax.rem(me, lows)

    def block(index):
        return pl.ds(pl.multiple_of(index * width, width), width)

    for e in range(lows):
        for d in range(groups):
            tiles = own[d] if e == 0 else others[e - 1].at[d]
            row = lax.rem(high + groups - d, groups) * lows + lax.rem(low + lows - e, lows)
            alive = live_ref[row]

            def term(s):
                left, right = tiles[s], virt_ref[block(cols_ref[row, s]), :]
                if s + 1 < slots:
                    second = jnp.where(s + 1 < alive, tiles[s + 1], jnp.zeros_like(left))
                    left = jnp.concatenate([left, second], axis=1)
                    right = jnp.concatenate([right, virt_ref[block(cols_ref[row, s + 1]), :]], axis=0)
                return jnp.dot(left, right, preferred_element_type=F32)

            steps = list(range(0, slots, 2))
            for n in range(len(steps)):
                here = alive > steps[n]
                if n + 1 < len(steps):
                    here = jnp.logical_and(here, alive <= steps[n + 1])

                @pl.when(here)
                def _():
                    total = term(steps[0])
                    for s in steps[1 : n + 1]:
                        total += term(s)
                    half[block(row), :] = total.astype(BF16)

    for d in range(groups):
        lhs[d * width : (d + 1) * width, :] = occ[(groups - d) % groups][...]
    wide = 2 * width
    for j in range(0, basis, wide):
        full[:, j : j + wide] = jnp.dot(
            lhs[...], half[:, j : j + wide], preferred_element_type=F32
        ).astype(BF16)
    for d in range(groups):
        row = lax.rem(high + d, groups) * lows + low
        alive = live_ref[row]
        for s in range(slots):
            tile = full[d * width : (d + 1) * width, block(cols_ref[row, s])]
            outs[d][s] = jnp.where(s < alive, tile, jnp.zeros_like(tile))


def polar(cols, live, virt, own, others, occ):
    groups, lows = len(own), len(others) + 1
    slots, width = own[0].shape[0], own[0].shape[1]
    basis = virt.shape[0]
    return pl.pallas_call(
        lambda *refs: polar_kernel(groups, lows, *refs),
        out_shape=[jax.ShapeDtypeStruct(own[0].shape, BF16)] * groups,
        in_specs=[SMEM, SMEM] + [VMEM] * (1 + len(own) + len(others) + len(occ)),
        out_specs=[VMEM] * groups,
        scratch_shapes=[
            pltpu.VMEM((basis, basis), BF16),
            pltpu.VMEM((groups * width, basis), BF16),
            pltpu.VMEM((groups * width, basis), BF16),
        ],
        compiler_params=pltpu.CompilerParams(vmem_limit_bytes=56 * 2**20),
        cost_estimate=pl.CostEstimate(
            flops=2 * basis * basis * (slots * width + groups * width),
            bytes_accessed=2 * basis * basis * 3,
            transcendentals=0,
        ),
        name="polar",
    )(cols, live, virt, *own, *others, *occ)


def chi_kernel(groups, lows, factor, all_ref, *rest):
    pieces, out = rest[:-1], rest[-1]
    count, rows, width = all_ref.shape
    high = lax.axis_index("pair") // lows
    step = 16
    total = jnp.zeros((count * step, len(pieces) * step), F32)
    for r in range(0, rows, 2 * step):

        def both(ref):
            return [ref[..., r + k * step : r + (k + 1) * step, :] for k in range(2)]

        left = jnp.concatenate([x.reshape(count * step, width) for x in both(all_ref)], axis=1)
        right = jnp.concatenate(
            [jnp.concatenate(both(ref), axis=1) for ref in pieces], axis=0
        )
        total += lax.dot_general(
            left, right, (((1,), (1,)), ((), ())), preferred_element_type=F32
        )
    row = lax.broadcasted_iota(jnp.int32, total.shape, 0) % step
    col = lax.broadcasted_iota(jnp.int32, total.shape, 1)
    total = jnp.where(row == col % step, total, 0.0).reshape(count, step, total.shape[1])
    total = jnp.sum(total, axis=1)
    group = lax.broadcasted_iota(jnp.int32, total.shape, 1) // step
    place = lax.broadcasted_iota(jnp.int32, out.shape, 1)
    result = jnp.zeros(out.shape, F32)
    for n in range(len(pieces)):
        c, d = divmod(n, groups)
        q = c * groups + lax.rem(high + groups - d, groups)
        value = jnp.sum(jnp.where(group == n, total, 0.0), axis=1, keepdims=True)
        result = jnp.where(place == q, value, result)
    out[...] = result * factor


def chi(everyone, pieces, groups, lows, factor):
    count, slots, width, _ = everyone.shape
    flat = [p.reshape(slots * width, width) for p in pieces]
    return pl.pallas_call(
        lambda *refs: chi_kernel(groups, lows, factor, *refs),
        out_shape=jax.ShapeDtypeStruct((count, len(pieces)), F32),
        in_specs=[VMEM] * (1 + len(pieces)),
        out_specs=VMEM,
        compiler_params=pltpu.CompilerParams(vmem_limit_bytes=56 * 2**20),
        cost_estimate=pl.CostEstimate(
            flops=2 * count * len(pieces) * slots * width * width,
            bytes_accessed=2 * (count + len(pieces)) * slots * width * width,
            transcendentals=0,
        ),
        name="chi",
    )(everyone.reshape(count, slots * width, width), *flat)


def per_device(three_centre, occ_green, virt_green, tile_cols, tile_live):
    local, slots, width, _ = three_centre.shape
    blocks = lax.axis_size("pair")
    groups = math.gcd(local, blocks)
    lows = blocks // groups
    chunks = local // groups

    def along_high(array, d):
        moves = [
            (h * lows + l, (h + d) % groups * lows + l) for h in range(groups) for l in range(lows)
        ]
        return lax.ppermute(array, "pair", moves)

    def along_low(array, e):
        moves = [
            (h * lows + l, h * lows + (l + e) % lows) for h in range(groups) for l in range(lows)
        ]
        return lax.ppermute(array, "pair", moves)

    pieces = split(three_centre, groups, lows)
    own = []
    for c in range(chunks):
        mine = pieces[c * groups : (c + 1) * groups]
        own.append([mine[0]] + [along_high(mine[d], d) for d in range(1, groups)])
        if c == 0:
            occ = [occ_green] + [along_high(occ_green, d) for d in range(1, groups)]
    everyone = lax.all_gather(three_centre, "aux", axis=0, tiled=True)
    back = []
    for c in range(chunks):
        stacked = jnp.stack(own[c])
        others = [along_low(stacked, e) for e in range(1, lows)]
        tiles = polar(tile_cols, tile_live, virt_green, own[c], others, occ)
        back += [tiles[0]] + [along_high(tiles[d], d) for d in range(1, groups)]
    factor = 1.0 / (width * math.sqrt(slots * blocks))
    part = chi(everyone, back, groups, lows, factor)
    part = part.reshape(blocks, -1, local)
    return jnp.sum(lax.all_to_all(part, "pair", 0, 0, tiled=True), axis=0)


def solution(mesh):
    placed = (P("aux", "pair", None, None), P("pair", None), P(), P(), P())
    return jax.shard_map(
        per_device, mesh=mesh, in_specs=placed, out_specs=P("pair", "aux"), check_vma=False
    )
```

```python
import math

import jax
import jax.numpy as jnp
from jax import lax
from jax.experimental import pallas as pl
from jax.experimental.pallas import tpu as pltpu
from jax.sharding import PartitionSpec as P

F32 = jnp.float32
BF16 = jnp.bfloat16
VMEM = pl.BlockSpec(memory_space=pltpu.VMEM)
SMEM = pl.BlockSpec(memory_space=pltpu.SMEM)
MIB = 2**20
QUICK = pl.CostEstimate(flops=0, bytes_accessed=2**20, transcendentals=0)
LONG = pl.CostEstimate(flops=2 * 10**11, bytes_accessed=2**28, transcendentals=0)


def size_of(shapes):
    return sum(math.prod(s.shape) * s.dtype.itemsize for s in shapes)


def rows_at(index, extent):
    return pl.ds(pl.multiple_of(index * extent, extent), extent)


def split_kernel(groups, lows, chunk, shares, copied, tiles_ref, *rest):
    high = lax.axis_index("pair") // lows
    slots, width = tiles_ref.shape[1], tiles_ref.shape[2]
    outs = rest if chunk else rest[1:]
    for d in range(groups):
        outs[d][0:slots] = tiles_ref[chunk * groups + lax.rem(high + d, groups)]
    if chunk == 0:
        occ_ref, part = rest[0], width // shares
        share = lax.axis_index("aux") if shares > 1 else 0
        for d in range(1, groups):
            for j in range(occ_ref.shape[1] // width):
                at = j * part
                outs[d][slots + at // width, at % width : at % width + part, :] = occ_ref[
                    rows_at(share, part), j * width : (j + 1) * width
                ]
    for out, (low, high) in zip(outs[groups:], copied):
        out[...] = tiles_ref[low:high]


def split(tiles, occ, groups, lows, chunk, shares, copied=()):
    _, slots, width, _ = tiles.shape
    extra = occ.shape[1] // (width * shares) if chunk == 0 else 0
    shapes = [
        jax.ShapeDtypeStruct((slots + (extra if d else 0), width, width), tiles.dtype)
        for d in range(groups)
    ]
    shapes += [jax.ShapeDtypeStruct((h - l,) + tiles.shape[1:], tiles.dtype) for l, h in copied]
    args = [tiles] if chunk else [tiles, occ]
    whole = lambda shape: pl.BlockSpec(shape, lambda _: (0,) * len(shape))
    specs = [whole(a.shape) for a in args]
    if chunk == 0:
        specs[0] = whole((groups,) + tiles.shape[1:])
    out = pl.pallas_call(
        lambda *refs: split_kernel(groups, lows, chunk, shares, copied, *refs),
        grid=(1,),
        out_shape=shapes,
        in_specs=specs,
        out_specs=[whole(s.shape) for s in shapes],
        cost_estimate=LONG,
        name="split",
    )(*args)
    return list(out[:groups]), list(out[groups:])


def stack_kernel(groups, slots, *refs):
    pieces, outs = refs[:groups], refs[groups:]
    for d, piece in enumerate(pieces):
        outs[0][d] = piece[0:slots]
        if len(outs) > 1 and d > 0:
            outs[1][d - 1] = piece[slots:]


def stack(pieces, slots, cost):
    groups, width = len(pieces), pieces[0].shape[1]
    extra = pieces[-1].shape[0] - slots
    shapes = [jax.ShapeDtypeStruct((groups, slots, width, width), BF16)]
    if extra:
        shapes.append(jax.ShapeDtypeStruct((groups - 1, extra, width, width), BF16))
    return pl.pallas_call(
        lambda *refs: stack_kernel(groups, slots, *refs),
        out_shape=shapes,
        in_specs=[VMEM] * groups,
        out_specs=[VMEM] * len(shapes),
        cost_estimate=cost,
        name="stack",
    )(*pieces)


def polar_kernel(groups, lows, masks, cols_ref, live_ref, virt_ref, occ_ref, *rest):
    rest = list(rest)
    take = lambda n: [rest.pop(0) for _ in range(n)]
    own, others, shares, outs = take(groups), take(lows - 1), take(len(masks)), take(groups)
    half, lhs, full = rest
    slots, width = outs[0].shape[0], outs[0].shape[1]
    basis = virt_ref.shape[0]
    me = lax.axis_index("pair")
    high, low = me // lows, lax.rem(me, lows)

    for e in range(lows):
        for d in range(groups):
            tiles = own[d] if e == 0 else others[e - 1].at[d]
            row = lax.rem(high + groups - d, groups) * lows + lax.rem(low + lows - e, lows)
            alive = live_ref[row]

            def term(s):
                left = tiles[s]
                right = virt_ref[rows_at(cols_ref[row, s], width), :]
                if s + 1 < slots:
                    second = jnp.where(s + 1 < alive, tiles[s + 1], jnp.zeros_like(left))
                    left = jnp.concatenate([left, second], axis=1)
                    below = virt_ref[rows_at(cols_ref[row, s + 1], width), :]
                    right = jnp.concatenate([right, below], axis=0)
                return jnp.dot(left, right, preferred_element_type=F32)

            steps = list(range(0, slots, 2))
            for n in range(len(steps)):
                here = alive > steps[n]
                if n + 1 < len(steps):
                    here = jnp.logical_and(here, alive <= steps[n + 1])

                @pl.when(here)
                def _():
                    total = term(steps[0])
                    for s in steps[1 : n + 1]:
                        total += term(s)
                    half[rows_at(row, width), :] = total.astype(BF16)

    lhs[0:width, :] = occ_ref[...]
    for mask_list, share in zip(masks, shares):
        part = width // (len(masks) * len(mask_list))
        for k, mask in enumerate(mask_list):
            source = lax.axis_index("aux") ^ mask if part < width else 0
            for d in range(1, groups):
                base = (groups - d) * width
                for j in range(basis // width):
                    at = j * part
                    lhs[
                        pl.ds(pl.multiple_of(base + source * part, part), part),
                        j * width : (j + 1) * width,
                    ] = share[k, d - 1, at // width, at % width : at % width + part, :]
    wide = 2 * width
    for j in range(0, basis, wide):
        full[:, j : j + wide] = jnp.dot(
            lhs[...], half[:, j : j + wide], preferred_element_type=F32
        ).astype(BF16)
    for d in range(groups):
        row = lax.rem(high + d, groups) * lows + low
        alive = live_ref[row]
        for s in range(slots):
            tile = full[d * width : (d + 1) * width, rows_at(cols_ref[row, s], width)]
            outs[d][s] = jnp.where(s < alive, tile, jnp.zeros_like(tile))


def polar(cols, live, virt, occ, own, others, masks, shares):
    groups, lows = len(own), len(others) + 1
    slots, width = own[0].shape[0], own[0].shape[1]
    basis = virt.shape[0]
    shapes = [jax.ShapeDtypeStruct((slots, width, width), BF16)] * groups
    scratch = [(basis, basis), (groups * width, basis), (groups * width, basis)]
    arrays = [virt, occ, *own, *others, *shares]
    held = size_of(arrays) + size_of(shapes) + sum(2 * a * b for a, b in scratch)
    return pl.pallas_call(
        lambda *refs: polar_kernel(groups, lows, masks, *refs),
        out_shape=shapes,
        in_specs=[SMEM, SMEM] + [VMEM] * len(arrays),
        out_specs=[VMEM] * groups,
        scratch_shapes=[pltpu.VMEM(s, BF16) for s in scratch],
        compiler_params=pltpu.CompilerParams(vmem_limit_bytes=held + 12 * MIB),
        cost_estimate=LONG,
        name="polar",
    )(cols, live, *arrays)


def chi_kernel(groups, lows, chunks, factor, places, *rest):
    count = groups * len(chunks)
    everyone, pieces = rest[: len(places)], rest[len(places) : len(places) + count]
    prior, out = rest[len(places) + count : -1], rest[-1]
    _, rows, width = everyone[0].shape
    unit, local = out.shape[1], out.shape[2]
    high, aux = lax.axis_index("pair") // lows, lax.axis_index("aux")
    step = 16

    def pair(ref, r):
        halves = [ref[..., r + k * step : r + (k + 1) * step, :] for k in range(2)]
        return jnp.concatenate([x.reshape(-1, width) for x in halves], axis=1)

    rights = [
        jnp.concatenate([pair(ref, r) for ref in pieces], axis=0) for r in range(0, rows, 2 * step)
    ]

    def product(ref):
        total = jnp.zeros((ref.shape[0] * step, count * step), F32)
        for right, r in zip(rights, range(0, rows, 2 * step)):
            total += lax.dot_general(
                pair(ref, r), right, (((1,), (1,)), ((), ())), preferred_element_type=F32
            )
        row = lax.broadcasted_iota(jnp.int32, total.shape, 0) % step
        col = lax.broadcasted_iota(jnp.int32, total.shape, 1) % step
        total = jnp.where(row == col, total, 0.0).reshape(-1, step, total.shape[1])
        return jnp.sum(total, axis=1)

    for mask in sorted({m for m, _ in places}):
        mine = sorted((start, n) for n, (m, start) in enumerate(places) if m == mask)
        total = [product(everyone[n]) for _, n in mine]
        total = jnp.concatenate(total, axis=0) if len(total) > 1 else total[0]
        group = lax.broadcasted_iota(jnp.int32, total.shape, 1) // step
        place = lax.broadcasted_iota(jnp.int32, (local, local), 1)
        result = jnp.zeros((local, local), F32)
        for n in range(count):
            c, d = divmod(n, groups)
            q = chunks[c] * groups + lax.rem(high + groups - d, groups)
            value = jnp.sum(jnp.where(group == n, total, 0.0), axis=1, keepdims=True)
            result = jnp.where(place == q, value * factor, result)
        for u in range(local // unit):
            at = (aux ^ mask) * (local // unit) + u
            piece = result[u * unit : (u + 1) * unit]
            out[at] = piece + prior[0][at] if prior else piece


def chi(everyone, back, chunks, prior, groups, lows, local, unit, factor):
    pieces = [p for c in chunks for p in back[c]]
    slots, width = pieces[0].shape[0], pieces[0].shape[1]
    places = [place for place, _ in everyone]
    arrays = [e.reshape(-1, slots * width, width) for _, e in everyone]
    arrays += [p.reshape(slots * width, width) for p in pieces]
    if prior is not None:
        arrays.append(prior)
    count = sum(e.shape[0] for _, e in everyone)
    return pl.pallas_call(
        lambda *refs: chi_kernel(groups, lows, chunks, factor, places, *refs),
        out_shape=jax.ShapeDtypeStruct((count // unit, unit, local), F32),
        in_specs=[VMEM] * len(arrays),
        out_specs=VMEM,
        compiler_params=pltpu.CompilerParams(vmem_limit_bytes=size_of(arrays) + 12 * MIB),
        cost_estimate=LONG,
        name="chi",
    )(*arrays)


def per_device(three_centre, occ_green, virt_green, tile_cols, tile_live):
    local, slots, width, _ = three_centre.shape
    blocks, peers = lax.axis_size("pair"), lax.axis_size("aux")
    groups = math.gcd(local, blocks)
    lows = blocks // groups
    chunks = local // groups
    shares = peers if peers & (peers - 1) == 0 and blocks % peers == 0 else 1

    def along_high(array, d):
        moves = [
            (h * lows + l, (h + d) % groups * lows + l) for h in range(groups) for l in range(lows)
        ]
        return lax.ppermute(array, "pair", moves)

    def along_low(array, e):
        moves = [
            (h * lows + l, h * lows + (l + e) % lows) for h in range(groups) for l in range(lows)
        ]
        return lax.ppermute(array, "pair", moves)

    def swap(array, bit):
        return lax.ppermute(array, "aux", [(a, a ^ bit) for a in range(peers)])

    def shift(arrays, between=lambda: None):
        order = sorted(range(1, groups), key=lambda d: -min(d, groups - d))
        moved = {0: arrays[0]}
        for d in order:
            moved[d] = along_high(arrays[d], d)
            if d == order[0]:
                between()
        return [moved[d] for d in range(groups)]

    together = lax.optimization_barrier
    factor = 1.0 / (width * math.sqrt(slots * blocks))
    bits = [1 << n for n in reversed(range(peers.bit_length() - 1))]
    own, others, tiles, back = {}, {}, {}, {}
    parts, masks = [], [[0]]
    everyone = [((0, 0), three_centre)]
    part, per = None, local * peers // blocks
    unit = math.gcd(local, per)

    first_back = max(chunks, 3)
    cut = -(-local * 7 // 12) if chunks > 1 else local
    first, copies = split(three_centre, occ_green, groups, lows, 0, shares)
    sending = {0: first}
    for phase in range(first_back + chunks):

        def share_low():
            if phase - 1 in own:
                stacked, *extra = stack(own[phase - 1], slots, QUICK if phase == chunks else LONG)
                if extra:
                    parts[:] = [extra[0][None]]
                others[phase - 1] = [along_low(stacked, e) for e in range(1, lows)]

        if phase in sending:
            own[phase] = shift(sending.pop(phase), share_low)
        elif phase >= first_back:
            back[phase - first_back] = shift(tiles.pop(phase - first_back), share_low)
        else:
            share_low()
        if phase in (1, 2):
            for bit in bits[: len(bits) - 1] if phase == 1 else bits[len(bits) - 1 :]:
                parts, masks = parts + [swap(x, bit) for x in parts], masks + [[m[0] | bit] for m in masks]
        if phase + 1 < chunks:
            sending[phase + 1], more = split(
                three_centre, occ_green, groups, lows, phase + 1, shares,
                [(0, cut)] * (phase == 0) + [(cut, local)] * (phase + 2 == chunks),
            )
            copies = copies + more
        if phase == 0 and bits:
            first_part = swap(copies[0] if copies else three_centre, bits[0])
            everyone.append(((bits[0], 0), first_part))
            if len(bits) > 1:
                everyone.append(((bits[-1], 0), swap(three_centre, bits[-1])))
        if phase == first_back - 1 and bits and cut < local:
            everyone.append(((bits[0], cut), swap(copies[1], bits[0])))
        if phase - 2 in others:
            c, pieces = phase - 2, own[phase - 2]
            if phase == first_back - 1 + 1 and everyone[-1][0][1]:
                pieces = together((pieces, everyone[-1][1]))[0]
            tiles[c] = list(
                polar(tile_cols, tile_live, virt_green, occ_green, pieces, others.pop(c), masks, parts)
            )
        if phase == first_back + chunks - 1:
            for bit in bits[1:]:
                for (mask, start), array in list(everyone):
                    if (mask ^ bit, start) not in dict(everyone):
                        array = together((array, back[chunks - 2]))[0]
                        everyone.append(((mask ^ bit, start), swap(array, bit)))
            if chunks > 1:
                part = chi(
                    everyone, back, list(range(chunks - 1)), None, groups, lows, local, unit, factor
                )
        done = {}
        if phase == 0 and len(bits) > 1:
            done[2] = everyone[2][1]
        if phase == 1 and bits:
            done[1] = everyone[1][1]
        live = (three_centre, sending, copies, own if phase < first_back else {}, tiles, back, parts, part, done)
        three_centre, sending, copies, kept, tiles, back, parts, part, done = together(live)
        own = kept or own
        for n, array in done.items():
            everyone[n] = (everyone[n][0], array)
    part = chi(everyone, back, [chunks - 1], part, groups, lows, local, unit, factor)
    part = part.reshape(blocks, per, local)
    return jnp.sum(lax.all_to_all(part, "pair", 0, 0, tiled=True), axis=0)


def solution(mesh):
    placed = (P("aux", "pair", None, None), P("pair", None), P(), P(), P())
    return jax.shard_map(
        per_device, mesh=mesh, in_specs=placed, out_specs=P("pair", "aux"), check_vma=False
    )
```

```python
import math

import jax
import jax.numpy as jnp
from jax import lax
from jax.experimental import pallas as pl
from jax.experimental.pallas import tpu as pltpu
from jax.sharding import PartitionSpec as P

F32 = jnp.float32
BF16 = jnp.bfloat16
VMEM = pl.BlockSpec(memory_space=pltpu.VMEM)
SMEM = pl.BlockSpec(memory_space=pltpu.SMEM)
MIB = 2**20
LONG = pl.CostEstimate(flops=2 * 10**11, bytes_accessed=2**20, transcendentals=0)
QUICK = pl.CostEstimate(flops=1, bytes_accessed=2**20, transcendentals=0)


def size_of(shapes):
    return sum(math.prod(s.shape) * s.dtype.itemsize for s in shapes)


def rows_at(index, extent):
    return pl.ds(pl.multiple_of(index * extent, extent), extent)


def split_kernel(groups, lows, chunk, shares, copied, tiles_ref, *rest):
    high = lax.axis_index("pair") // lows
    slots, width = tiles_ref.shape[1], tiles_ref.shape[2]
    outs = rest if chunk else rest[1:]
    for d in range(groups):
        outs[d][0:slots] = tiles_ref[chunk * groups + lax.rem(high + d, groups)]
    if chunk == 0:
        occ_ref, part = rest[0], width // shares
        share = lax.axis_index("aux") if shares > 1 else 0
        for d in range(1, groups):
            for j in range(occ_ref.shape[1] // width):
                at = j * part
                outs[d][slots + at // width, at % width : at % width + part, :] = occ_ref[
                    rows_at(share, part), j * width : (j + 1) * width
                ]
    for out, (low, high) in zip(outs[groups:], copied):
        out[...] = tiles_ref[low:high]


def split(tiles, occ, groups, lows, chunk, shares, copied=()):
    _, slots, width, _ = tiles.shape
    extra = occ.shape[1] // (width * shares) if chunk == 0 else 0
    shapes = [
        jax.ShapeDtypeStruct((slots + (extra if d else 0), width, width), tiles.dtype)
        for d in range(groups)
    ]
    shapes += [jax.ShapeDtypeStruct((h - l,) + tiles.shape[1:], tiles.dtype) for l, h in copied]
    args = [tiles] if chunk else [tiles, occ]
    whole = lambda shape: pl.BlockSpec(shape, lambda _: (0,) * len(shape))
    specs = [whole(a.shape) for a in args]
    if chunk == 0:
        specs[0] = whole((groups,) + tiles.shape[1:])
    out = pl.pallas_call(
        lambda *refs: split_kernel(groups, lows, chunk, shares, copied, *refs),
        grid=(1,),
        out_shape=shapes,
        in_specs=specs,
        out_specs=[whole(s.shape) for s in shapes],
        cost_estimate=LONG,
        name="split",
    )(*args)
    return list(out[:groups]), list(out[groups:])


def stack_kernel(groups, slots, *refs):
    pieces, outs = refs[:groups], refs[groups:]
    for d, piece in enumerate(pieces):
        outs[0][d] = piece[0:slots]
        if len(outs) > 1 and d > 0:
            outs[1][d - 1] = piece[slots:]


def stack(pieces, slots, cost):
    groups, width = len(pieces), pieces[0].shape[1]
    extra = pieces[-1].shape[0] - slots
    shapes = [jax.ShapeDtypeStruct((groups, slots, width, width), BF16)]
    if extra:
        shapes.append(jax.ShapeDtypeStruct((groups - 1, extra, width, width), BF16))
    return pl.pallas_call(
        lambda *refs: stack_kernel(groups, slots, *refs),
        out_shape=shapes,
        in_specs=[VMEM] * groups,
        out_specs=[VMEM] * len(shapes),
        cost_estimate=cost,
        name="stack",
    )(*pieces)


def polar_kernel(groups, lows, masks, cols_ref, live_ref, virt_ref, occ_ref, *rest):
    rest = list(rest)
    take = lambda n: [rest.pop(0) for _ in range(n)]
    own, others, shares, outs = take(groups), take(lows - 1), take(len(masks)), take(groups)
    dense, lhs, half, full = rest
    slots, width = outs[0].shape[0], outs[0].shape[1]
    basis = virt_ref.shape[0]
    me = lax.axis_index("pair")
    high, low = me // lows, lax.rem(me, lows)

    dense[...] = jnp.zeros_like(dense)
    for e in range(lows):
        for d in range(groups):
            tiles = own[d] if e == 0 else others[e - 1].at[d]
            row = lax.rem(high + groups - d, groups) * lows + lax.rem(low + lows - e, lows)
            for s in range(slots):

                @pl.when(s < live_ref[row])
                def _():
                    dense[rows_at(row, width), rows_at(cols_ref[row, s], width)] = tiles[s]

    lhs[0:width, :] = occ_ref[...]
    for mask_list, share in zip(masks, shares):
        part = width // (len(masks) * len(mask_list))
        for k, mask in enumerate(mask_list):
            source = lax.axis_index("aux") ^ mask if part < width else 0
            for d in range(1, groups):
                base = (groups - d) * width
                for j in range(basis // width):
                    at = j * part
                    lhs[
                        pl.ds(pl.multiple_of(base + source * part, part), part),
                        j * width : (j + 1) * width,
                    ] = share[k, d - 1, at // width, at % width : at % width + part, :]
    wide = 2 * width
    for source, by, into in ((lhs, dense, half), (half, virt_ref, full)):
        for j in range(0, basis, wide):
            into[:, j : j + wide] = jnp.dot(
                source[...], by[:, j : j + wide], preferred_element_type=F32
            ).astype(BF16)
    for d in range(groups):
        row = lax.rem(high + d, groups) * lows + low
        alive = live_ref[row]
        for s in range(slots):
            tile = full[d * width : (d + 1) * width, rows_at(cols_ref[row, s], width)]
            outs[d][s] = jnp.where(s < alive, tile, jnp.zeros_like(tile))


def polar(cols, live, virt, occ, own, others, masks, shares):
    groups, lows = len(own), len(others) + 1
    slots, width = own[0].shape[0], own[0].shape[1]
    basis = virt.shape[0]
    shapes = [jax.ShapeDtypeStruct((slots, width, width), BF16)] * groups
    scratch = [(basis, basis)] + [(groups * width, basis)] * 3
    arrays = [virt, occ, *own, *others, *shares]
    held = size_of(arrays) + size_of(shapes) + sum(2 * a * b for a, b in scratch)
    return pl.pallas_call(
        lambda *refs: polar_kernel(groups, lows, masks, *refs),
        out_shape=shapes,
        in_specs=[SMEM, SMEM] + [VMEM] * len(arrays),
        out_specs=[VMEM] * groups,
        scratch_shapes=[pltpu.VMEM(s, BF16) for s in scratch],
        compiler_params=pltpu.CompilerParams(vmem_limit_bytes=held + 12 * MIB),
        cost_estimate=LONG,
        name="polar",
    )(cols, live, *arrays)


def chi_kernel(groups, lows, chunks, factor, places, keep, *rest):
    count = groups * len(chunks)
    everyone, pieces = rest[: len(places)], rest[len(places) : len(places) + count]
    kept = rest[len(rest) - len(places) :] if keep else ()
    prior, out = rest[len(places) + count : -1 - len(kept)], rest[-1 - len(kept)]
    for ref, copy in zip(everyone, kept):
        copy[...] = ref[...]
    _, rows, width = everyone[0].shape
    unit, local = out.shape[1], out.shape[2]
    high, aux = lax.axis_index("pair") // lows, lax.axis_index("aux")
    step = 16

    def pair(ref, r):
        halves = [ref[..., r + k * step : r + (k + 1) * step, :] for k in range(2)]
        return jnp.concatenate([x.reshape(-1, width) for x in halves], axis=1)

    rights = [
        jnp.concatenate([pair(ref, r) for ref in pieces], axis=0) for r in range(0, rows, 2 * step)
    ]

    def product(ref):
        total = jnp.zeros((ref.shape[0] * step, count * step), F32)
        for right, r in zip(rights, range(0, rows, 2 * step)):
            total += lax.dot_general(
                pair(ref, r), right, (((1,), (1,)), ((), ())), preferred_element_type=F32
            )
        row = lax.broadcasted_iota(jnp.int32, total.shape, 0) % step
        col = lax.broadcasted_iota(jnp.int32, total.shape, 1) % step
        total = jnp.where(row == col, total, 0.0).reshape(-1, step, total.shape[1])
        return jnp.sum(total, axis=1)

    for mask in sorted({m for m, _ in places}):
        mine = sorted((start, n) for n, (m, start) in enumerate(places) if m == mask)
        total = [product(everyone[n]) for _, n in mine]
        total = jnp.concatenate(total, axis=0) if len(total) > 1 else total[0]
        group = lax.broadcasted_iota(jnp.int32, total.shape, 1) // step
        place = lax.broadcasted_iota(jnp.int32, (local, local), 1)
        result = jnp.zeros((local, local), F32)
        for n in range(count):
            c, d = divmod(n, groups)
            q = chunks[c] * groups + lax.rem(high + groups - d, groups)
            value = jnp.sum(jnp.where(group == n, total, 0.0), axis=1, keepdims=True)
            result = jnp.where(place == q, value * factor, result)
        for u in range(local // unit):
            at = (aux ^ mask) * (local // unit) + u
            piece = result[u * unit : (u + 1) * unit]
            out[at] = piece + prior[0][at] if prior else piece


def chi(everyone, back, chunks, prior, groups, lows, local, unit, factor, keep=False):
    pieces = [p for c in chunks for p in back[c]]
    slots, width = pieces[0].shape[0], pieces[0].shape[1]
    places = [place for place, _ in everyone]
    arrays = [e.reshape(-1, slots * width, width) for _, e in everyone]
    arrays += [p.reshape(slots * width, width) for p in pieces]
    if prior is not None:
        arrays.append(prior)
    count = sum(e.shape[0] for _, e in everyone)
    part, *kept = pl.pallas_call(
        lambda *refs: chi_kernel(groups, lows, chunks, factor, places, keep, *refs),
        out_shape=[jax.ShapeDtypeStruct((count // unit, unit, local), F32)]
        + [pltpu.VMEM(a.shape, a.dtype) for a in arrays[: len(places)] if keep],
        in_specs=[VMEM] * len(arrays),
        out_specs=[VMEM] * (1 + len(places) * keep),
        compiler_params=pltpu.CompilerParams(vmem_limit_bytes=size_of(arrays) + 12 * MIB),
        cost_estimate=LONG,
        name="chi",
    )(*arrays)
    return part, [(place, e) for place, e in zip(places, kept)] if keep else everyone


def per_device(three_centre, occ_green, virt_green, tile_cols, tile_live):
    local, slots, width, _ = three_centre.shape
    blocks, peers = lax.axis_size("pair"), lax.axis_size("aux")
    groups = math.gcd(local, blocks)
    lows = blocks // groups
    chunks = local // groups
    shares = peers if peers & (peers - 1) == 0 and blocks % peers == 0 else 1

    def along_high(array, d):
        moves = [
            (h * lows + l, (h + d) % groups * lows + l) for h in range(groups) for l in range(lows)
        ]
        return lax.ppermute(array, "pair", moves)

    def along_low(array, e):
        moves = [
            (h * lows + l, h * lows + (l + e) % lows) for h in range(groups) for l in range(lows)
        ]
        return lax.ppermute(array, "pair", moves)

    def swap(array, bit):
        return lax.ppermute(array, "aux", [(a, a ^ bit) for a in range(peers)])

    def shift(arrays, between=lambda: None):
        order = sorted(range(1, groups), key=lambda d: -min(d, groups - d))
        moved = {0: arrays[0]}
        for d in order:
            moved[d] = along_high(arrays[d], d)
            if d == order[0]:
                between()
        return [moved[d] for d in range(groups)]

    together = lax.optimization_barrier
    factor = 1.0 / (width * math.sqrt(slots * blocks))
    bits = [1 << n for n in reversed(range(peers.bit_length() - 1))]
    own, others, tiles, back = {}, {}, {}, {}
    parts, masks = [], [[0]]
    everyone = [((0, 0), three_centre)]
    part, per = None, local * peers // blocks
    unit = math.gcd(local, per)

    first_back = max(chunks, 3)
    cut = -(-local * 7 // 12) if chunks > 1 else local
    first, copies = split(three_centre, occ_green, groups, lows, 0, shares)
    sending = {0: first}
    for phase in range(first_back + chunks):

        def share_low():
            if phase - 1 in own:
                stacked, *extra = stack(own[phase - 1], slots, QUICK if phase == chunks else LONG)
                if extra:
                    parts[:] = [extra[0][None]]
                others[phase - 1] = [along_low(stacked, e) for e in range(1, lows)]

        if phase in sending:
            own[phase] = shift(sending.pop(phase), share_low)
        elif phase >= first_back:
            back[phase - first_back] = shift(tiles.pop(phase - first_back), share_low)
        else:
            share_low()
        if phase in (1, 2):
            for bit in bits[: len(bits) - 1] if phase == 1 else bits[len(bits) - 1 :]:
                parts, masks = parts + [swap(x, bit) for x in parts], masks + [[m[0] | bit] for m in masks]
        for c in range(1, chunks):
            if phase == c - 1:
                runs = ([(0, cut)] * (c == 1) + [(cut, local)] * (c == chunks - 1)) * (cut < local)
                sending[c], more = split(three_centre, occ_green, groups, lows, c, shares, runs)
                copies = copies + more
        if phase == 0 and bits:
            first_part = swap(copies[0] if copies else three_centre, bits[0])
            everyone.append(((bits[0], 0), first_part))
            if len(bits) > 1:
                everyone.append(((bits[-1], 0), swap(three_centre, bits[-1])))
        if phase == first_back - 1 and bits and cut < local:
            everyone.append(((bits[0], cut), swap(copies[1], bits[0])))
        if phase - 2 in others:
            c, pieces = phase - 2, own[phase - 2]
            if phase == first_back - 1 + 1 and everyone[-1][0][1]:
                pieces = together((pieces, everyone[-1][1]))[0]
            tiles[c] = list(
                polar(tile_cols, tile_live, virt_green, occ_green, pieces, others.pop(c), masks, parts)
            )
        if phase == first_back + chunks - 1:
            for bit in bits[1:]:
                for (mask, start), array in list(everyone):
                    if (mask ^ bit, start) not in dict(everyone):
                        array = together((array, back[chunks - 2]))[0]
                        everyone.append(((mask ^ bit, start), swap(array, bit)))
            if chunks > 1:
                part, everyone = chi(
                    everyone, back, list(range(chunks - 1)), None, groups, lows, local, unit, factor, True
                )
        done = {}
        if phase == 0 and len(bits) > 1:
            done[2] = everyone[2][1]
        if phase == 1 and bits:
            done[1] = everyone[1][1]
        live = (three_centre, sending, copies, own if phase < first_back else {}, tiles, back, parts, part, done)
        three_centre, sending, copies, kept, tiles, back, parts, part, done = together(live)
        own = kept or own
        for n, array in done.items():
            everyone[n] = (everyone[n][0], array)
    part, _ = chi(everyone, back, [chunks - 1], part, groups, lows, local, unit, factor)
    part = part.reshape(blocks, per, local)
    return jnp.sum(lax.all_to_all(part, "pair", 0, 0, tiled=True), axis=0)


def solution(mesh):
    placed = (P("aux", "pair", None, None), P("pair", None), P(), P(), P())
    return jax.shard_map(
        per_device, mesh=mesh, in_specs=placed, out_specs=P("pair", "aux"), check_vma=False
    )
```

```python
import math

import jax
import jax.numpy as jnp
from jax import lax
from jax.experimental import pallas as pl
from jax.experimental.pallas import tpu as pltpu
from jax.sharding import PartitionSpec as P

F32 = jnp.float32
BF16 = jnp.bfloat16
VMEM = pl.BlockSpec(memory_space=pltpu.VMEM)
SMEM = pl.BlockSpec(memory_space=pltpu.SMEM)
MIB = 2**20
LONG = pl.CostEstimate(flops=2 * 10**11, bytes_accessed=2**20, transcendentals=0)
QUICK = pl.CostEstimate(flops=1, bytes_accessed=2**20, transcendentals=0)


def size_of(shapes):
    return sum(math.prod(s.shape) * s.dtype.itemsize for s in shapes)


def rows_at(index, extent):
    return pl.ds(pl.multiple_of(index * extent, extent), extent)


def split_kernel(groups, lows, chunk, shares, copied, tiles_ref, *rest):
    high = lax.axis_index("pair") // lows
    slots, width = tiles_ref.shape[1], tiles_ref.shape[2]
    outs = rest if chunk else rest[1:]
    for d in range(groups):
        outs[d][0:slots] = tiles_ref[chunk * groups + lax.rem(high + d, groups)]
    if chunk == 0:
        occ_ref, part = rest[0], width // shares
        share = lax.axis_index("aux") if shares > 1 else 0
        for d in range(1, groups):
            for j in range(occ_ref.shape[1] // width):
                at = j * part
                outs[d][slots + at // width, at % width : at % width + part, :] = occ_ref[
                    rows_at(share, part), j * width : (j + 1) * width
                ]
    for out, (low, high) in zip(outs[groups:], copied):
        out[...] = tiles_ref[low:high]


def split(tiles, occ, groups, lows, chunk, shares, copied=()):
    _, slots, width, _ = tiles.shape
    extra = occ.shape[1] // (width * shares) if chunk == 0 else 0
    shapes = [
        jax.ShapeDtypeStruct((slots + (extra if d else 0), width, width), tiles.dtype)
        for d in range(groups)
    ]
    shapes += [jax.ShapeDtypeStruct((h - l,) + tiles.shape[1:], tiles.dtype) for l, h in copied]
    args = [tiles] if chunk else [tiles, occ]
    whole = lambda shape: pl.BlockSpec(shape, lambda _: (0,) * len(shape))
    specs = [whole(a.shape) for a in args]
    if chunk == 0:
        specs[0] = whole((groups,) + tiles.shape[1:])
    out = pl.pallas_call(
        lambda *refs: split_kernel(groups, lows, chunk, shares, copied, *refs),
        grid=(1,),
        out_shape=shapes,
        in_specs=specs,
        out_specs=[whole(s.shape) for s in shapes],
        cost_estimate=LONG,
        name="split",
    )(*args)
    return list(out[:groups]), list(out[groups:])


def stack_kernel(groups, slots, *refs):
    pieces, outs = refs[:groups], refs[groups:]
    for d, piece in enumerate(pieces):
        outs[0][d] = piece[0:slots]
        if len(outs) > 1 and d > 0:
            outs[1][d - 1] = piece[slots:]


def stack(pieces, slots, cost):
    groups, width = len(pieces), pieces[0].shape[1]
    extra = pieces[-1].shape[0] - slots
    shapes = [jax.ShapeDtypeStruct((groups, slots, width, width), BF16)]
    if extra:
        shapes.append(jax.ShapeDtypeStruct((groups - 1, extra, width, width), BF16))
    return pl.pallas_call(
        lambda *refs: stack_kernel(groups, slots, *refs),
        out_shape=shapes,
        in_specs=[VMEM] * groups,
        out_specs=[VMEM] * len(shapes),
        cost_estimate=cost,
        name="stack",
    )(*pieces)


def polar_kernel(groups, lows, masks, cols_ref, live_ref, virt_ref, occ_ref, *rest):
    rest = list(rest)
    take = lambda n: [rest.pop(0) for _ in range(n)]
    own, others, shares, outs = take(groups), take(lows - 1), take(len(masks)), take(groups)
    dense, lhs, half, full = rest
    slots, width = outs[0].shape[0], outs[0].shape[1]
    basis = virt_ref.shape[0]
    me = lax.axis_index("pair")
    high, low = me // lows, lax.rem(me, lows)

    dense[...] = jnp.zeros_like(dense)
    for e in range(lows):
        for d in range(groups):
            tiles = own[d] if e == 0 else others[e - 1].at[d]
            row = lax.rem(high + groups - d, groups) * lows + lax.rem(low + lows - e, lows)
            for s in range(slots):

                @pl.when(s < live_ref[row])
                def _():
                    dense[rows_at(row, width), rows_at(cols_ref[row, s], width)] = tiles[s]

    lhs[0:width, :] = occ_ref[...]
    for mask_list, share in zip(masks, shares):
        part = width // (len(masks) * len(mask_list))
        for k, mask in enumerate(mask_list):
            source = lax.axis_index("aux") ^ mask if part < width else 0
            for d in range(1, groups):
                base = (groups - d) * width
                for j in range(basis // width):
                    at = j * part
                    lhs[
                        pl.ds(pl.multiple_of(base + source * part, part), part),
                        j * width : (j + 1) * width,
                    ] = share[k, d - 1, at // width, at % width : at % width + part, :]
    wide = 2 * width
    for source, by, into in ((lhs, dense, half), (half, virt_ref, full)):
        for j in range(0, basis, wide):
            into[:, j : j + wide] = jnp.dot(
                source[...], by[:, j : j + wide], preferred_element_type=F32
            ).astype(BF16)
    for d in range(groups):
        row = lax.rem(high + d, groups) * lows + low
        alive = live_ref[row]
        for s in range(slots):
            tile = full[d * width : (d + 1) * width, rows_at(cols_ref[row, s], width)]
            outs[d][s] = jnp.where(s < alive, tile, jnp.zeros_like(tile))


def polar(cols, live, virt, occ, own, others, masks, shares):
    groups, lows = len(own), len(others) + 1
    slots, width = own[0].shape[0], own[0].shape[1]
    basis = virt.shape[0]
    shapes = [jax.ShapeDtypeStruct((slots, width, width), BF16)] * groups
    scratch = [(basis, basis)] + [(groups * width, basis)] * 3
    arrays = [virt, occ, *own, *others, *shares]
    held = size_of(arrays) + size_of(shapes) + sum(2 * a * b for a, b in scratch)
    return pl.pallas_call(
        lambda *refs: polar_kernel(groups, lows, masks, *refs),
        out_shape=shapes,
        in_specs=[SMEM, SMEM] + [VMEM] * len(arrays),
        out_specs=[VMEM] * groups,
        scratch_shapes=[pltpu.VMEM(s, BF16) for s in scratch],
        compiler_params=pltpu.CompilerParams(vmem_limit_bytes=held + 12 * MIB),
        cost_estimate=LONG,
        name="polar",
    )(cols, live, *arrays)


def chi_kernel(groups, lows, chunks, factor, places, keep, *rest):
    count = groups * len(chunks)
    everyone, pieces = rest[: len(places)], rest[len(places) : len(places) + count]
    kept = rest[len(rest) - len(places) :] if keep else ()
    prior, out = rest[len(places) + count : -1 - len(kept)], rest[-1 - len(kept)]
    for ref, copy in zip(everyone, kept):
        copy[...] = ref[...]
    _, rows, width = everyone[0].shape
    unit, local = out.shape[1], out.shape[2]
    high, aux = lax.axis_index("pair") // lows, lax.axis_index("aux")
    step = 16

    def pair(ref, r):
        halves = [ref[..., r + k * step : r + (k + 1) * step, :] for k in range(2)]
        return jnp.concatenate([x.reshape(-1, width) for x in halves], axis=1)

    rights = [
        jnp.concatenate([pair(ref, r) for ref in pieces], axis=0) for r in range(0, rows, 2 * step)
    ]

    def product(ref):
        total = jnp.zeros((ref.shape[0] * step, count * step), F32)
        for right, r in zip(rights, range(0, rows, 2 * step)):
            total += lax.dot_general(
                pair(ref, r), right, (((1,), (1,)), ((), ())), preferred_element_type=F32
            )
        row = lax.broadcasted_iota(jnp.int32, total.shape, 0) % step
        col = lax.broadcasted_iota(jnp.int32, total.shape, 1) % step
        total = jnp.where(row == col, total, 0.0).reshape(-1, step, total.shape[1])
        return jnp.sum(total, axis=1)

    for mask in sorted({m for m, _ in places}):
        mine = sorted((start, n) for n, (m, start) in enumerate(places) if m == mask)
        total = [product(everyone[n]) for _, n in mine]
        total = jnp.concatenate(total, axis=0) if len(total) > 1 else total[0]
        group = lax.broadcasted_iota(jnp.int32, total.shape, 1) // step
        place = lax.broadcasted_iota(jnp.int32, (local, local), 1)
        result = jnp.zeros((local, local), F32)
        for n in range(count):
            c, d = divmod(n, groups)
            q = chunks[c] * groups + lax.rem(high + groups - d, groups)
            value = jnp.sum(jnp.where(group == n, total, 0.0), axis=1, keepdims=True)
            result = jnp.where(place == q, value * factor, result)
        for u in range(local // unit):
            at = (aux ^ mask) * (local // unit) + u
            piece = result[u * unit : (u + 1) * unit]
            out[at] = piece + prior[0][at] if prior else piece


def chi(everyone, back, chunks, prior, groups, lows, local, unit, factor, keep=False):
    pieces = [p for c in chunks for p in back[c]]
    slots, width = pieces[0].shape[0], pieces[0].shape[1]
    places = [place for place, _ in everyone]
    arrays = [e.reshape(-1, slots * width, width) for _, e in everyone]
    arrays += [p.reshape(slots * width, width) for p in pieces]
    if prior is not None:
        arrays.append(prior)
    count = sum(e.shape[0] for _, e in everyone)
    part, *kept = pl.pallas_call(
        lambda *refs: chi_kernel(groups, lows, chunks, factor, places, keep, *refs),
        out_shape=[jax.ShapeDtypeStruct((count // unit, unit, local), F32)]
        + [pltpu.VMEM(a.shape, a.dtype) for a in arrays[: len(places)] if keep],
        in_specs=[VMEM] * len(arrays),
        out_specs=[VMEM] * (1 + len(places) * keep),
        compiler_params=pltpu.CompilerParams(vmem_limit_bytes=size_of(arrays) + 12 * MIB),
        cost_estimate=LONG,
        name="chi",
    )(*arrays)
    return part, [(place, e) for place, e in zip(places, kept)] if keep else everyone


def per_device(three_centre, occ_green, virt_green, tile_cols, tile_live):
    local, slots, width, _ = three_centre.shape
    blocks, peers = lax.axis_size("pair"), lax.axis_size("aux")
    groups = math.gcd(local, blocks)
    lows = blocks // groups
    chunks = local // groups
    shares = peers if peers & (peers - 1) == 0 and blocks % peers == 0 else 1

    def along_high(array, d):
        moves = [
            (h * lows + l, (h + d) % groups * lows + l) for h in range(groups) for l in range(lows)
        ]
        return lax.ppermute(array, "pair", moves)

    def along_low(array, e):
        moves = [
            (h * lows + l, h * lows + (l + e) % lows) for h in range(groups) for l in range(lows)
        ]
        return lax.ppermute(array, "pair", moves)

    def swap(array, bit):
        return lax.ppermute(array, "aux", [(a, a ^ bit) for a in range(peers)])

    def shift(arrays, between=lambda: None):
        order = sorted(range(1, groups), key=lambda d: (min(d, groups - d), -d))
        moved = {0: arrays[0]}
        for d in order:
            moved[d] = along_high(arrays[d], d)
            if d == order[-1]:
                between()
        return [moved[d] for d in range(groups)]

    together = lax.optimization_barrier
    factor = 1.0 / (width * math.sqrt(slots * blocks))
    bits = [1 << n for n in reversed(range(peers.bit_length() - 1))]
    own, others, tiles, back = {}, {}, {}, {}
    parts, masks = [], [[0]]
    everyone = [((0, 0), three_centre)]
    part, per = None, local * peers // blocks
    unit = math.gcd(local, per)

    first_back = max(chunks, 3)
    cut = -(-local * 7 // 12) if chunks > 1 else local
    first, copies = split(three_centre, occ_green, groups, lows, 0, shares)
    sending = {0: first}
    for phase in range(first_back + chunks):

        def share_low():
            if phase - 1 in own:
                stacked, *extra = stack(own[phase - 1], slots, QUICK if phase == chunks else LONG)
                if extra:
                    parts[:] = [extra[0][None]]
                others[phase - 1] = [along_low(stacked, e) for e in range(1, lows)]

        if phase in sending:
            own[phase] = shift(sending.pop(phase), share_low)
        elif phase >= first_back:
            back[phase - first_back] = shift(tiles.pop(phase - first_back), share_low)
        else:
            share_low()
        if phase in (1, 2):
            for bit in bits[: len(bits) - 1] if phase == 1 else bits[len(bits) - 1 :]:
                parts, masks = parts + [swap(x, bit) for x in parts], masks + [[m[0] | bit] for m in masks]
        for c in range(1, chunks):
            if phase == c - 1:
                runs = ([(0, cut)] * (c == 1) + [(cut, local)] * (c == chunks - 1)) * (cut < local)
                sending[c], more = split(three_centre, occ_green, groups, lows, c, shares, runs)
                copies = copies + more
        if phase == 0 and bits:
            first_part = swap(copies[0] if copies else three_centre, bits[0])
            everyone.append(((bits[0], 0), first_part))
            if len(bits) > 1:
                everyone.append(((bits[-1], 0), swap(three_centre, bits[-1])))
        if phase == first_back - 1 and bits and cut < local:
            everyone.append(((bits[0], cut), swap(copies[1], bits[0])))
        if phase - 2 in others:
            c, pieces = phase - 2, own[phase - 2]
            if phase == first_back - 1 + 1 and everyone[-1][0][1]:
                pieces = together((pieces, everyone[-1][1]))[0]
            tiles[c] = list(
                polar(tile_cols, tile_live, virt_green, occ_green, pieces, others.pop(c), masks, parts)
            )
        if phase == first_back + chunks - 1:
            for bit in bits[1:]:
                for (mask, start), array in list(everyone):
                    if (mask ^ bit, start) not in dict(everyone):
                        array = together((array, back[chunks - 2]))[0]
                        everyone.append(((mask ^ bit, start), swap(array, bit)))
            if chunks > 1:
                part, everyone = chi(
                    everyone, back, list(range(chunks - 1)), None, groups, lows, local, unit, factor, True
                )
        done = {}
        if phase == 0 and len(bits) > 1:
            done[2] = everyone[2][1]
        if phase == 1 and bits:
            done[1] = everyone[1][1]
        live = (three_centre, sending, copies, own if phase < first_back else {}, tiles, back, parts, part, done)
        three_centre, sending, copies, kept, tiles, back, parts, part, done = together(live)
        own = kept or own
        for n, array in done.items():
            everyone[n] = (everyone[n][0], array)
    part, _ = chi(everyone, back, [chunks - 1], part, groups, lows, local, unit, factor)
    part = part.reshape(blocks, per, local)
    return jnp.sum(lax.all_to_all(part, "pair", 0, 0, tiled=True), axis=0)


def solution(mesh):
    placed = (P("aux", "pair", None, None), P("pair", None), P(), P(), P())
    return jax.shard_map(
        per_device, mesh=mesh, in_specs=placed, out_specs=P("pair", "aux"), check_vma=False
    )
```

```python
import math

import jax
import jax.numpy as jnp
from jax import lax
from jax.experimental import pallas as pl
from jax.experimental.pallas import tpu as pltpu
from jax.sharding import PartitionSpec as P

F32 = jnp.float32
BF16 = jnp.bfloat16
VMEM = pl.BlockSpec(memory_space=pltpu.VMEM)
SMEM = pl.BlockSpec(memory_space=pltpu.SMEM)
MIB = 2**20
LONG = pl.CostEstimate(flops=2 * 10**11, bytes_accessed=2**20, transcendentals=0)
MIDDLE = pl.CostEstimate(flops=5 * 10**9, bytes_accessed=2**20, transcendentals=0)
QUICK = pl.CostEstimate(flops=1, bytes_accessed=2**20, transcendentals=0)


def size_of(shapes):
    return sum(math.prod(s.shape) * s.dtype.itemsize for s in shapes)


def rows_at(index, extent):
    return pl.ds(pl.multiple_of(index * extent, extent), extent)


def split_kernel(groups, lows, chunk, shares, copied, tiles_ref, *rest):
    high = lax.axis_index("pair") // lows
    slots, width = tiles_ref.shape[1], tiles_ref.shape[2]
    outs = rest if chunk else rest[1:]
    for d in range(groups):
        outs[d][0:slots] = tiles_ref[chunk * groups + lax.rem(high + d, groups)]
    if chunk == 0:
        occ_ref, part = rest[0], width // shares
        share = lax.axis_index("aux") if shares > 1 else 0
        for d in range(1, groups):
            for j in range(occ_ref.shape[1] // width):
                at = j * part
                outs[d][slots + at // width, at % width : at % width + part, :] = occ_ref[
                    rows_at(share, part), j * width : (j + 1) * width
                ]
    for out, (low, high) in zip(outs[groups:], copied):
        out[...] = tiles_ref[low:high]


def split(tiles, occ, groups, lows, chunk, shares, copied=()):
    _, slots, width, _ = tiles.shape
    extra = occ.shape[1] // (width * shares) if chunk == 0 else 0
    shapes = [
        jax.ShapeDtypeStruct((slots + (extra if d else 0), width, width), tiles.dtype)
        for d in range(groups)
    ]
    shapes += [jax.ShapeDtypeStruct((h - l,) + tiles.shape[1:], tiles.dtype) for l, h in copied]
    args = [tiles] if chunk else [tiles, occ]
    whole = lambda shape: pl.BlockSpec(shape, lambda _: (0,) * len(shape))
    specs = [whole(a.shape) for a in args]
    if chunk == 0:
        specs[0] = whole((groups,) + tiles.shape[1:])
    out = pl.pallas_call(
        lambda *refs: split_kernel(groups, lows, chunk, shares, copied, *refs),
        grid=(1,),
        out_shape=shapes,
        in_specs=specs,
        out_specs=[whole(s.shape) for s in shapes],
        cost_estimate=LONG,
        name="split",
    )(*args)
    return list(out[:groups]), list(out[groups:])


def stack_kernel(groups, slots, *refs):
    pieces, outs = refs[:groups], refs[groups:]
    for d, piece in enumerate(pieces):
        outs[0][d] = piece[0:slots]
        if len(outs) > 1 and d > 0:
            outs[1][d - 1] = piece[slots:]


def stack(pieces, slots, cost):
    groups, width = len(pieces), pieces[0].shape[1]
    extra = pieces[-1].shape[0] - slots
    shapes = [jax.ShapeDtypeStruct((groups, slots, width, width), BF16)]
    if extra:
        shapes.append(jax.ShapeDtypeStruct((groups - 1, extra, width, width), BF16))
    return pl.pallas_call(
        lambda *refs: stack_kernel(groups, slots, *refs),
        out_shape=shapes,
        in_specs=[VMEM] * groups,
        out_specs=[VMEM] * len(shapes),
        cost_estimate=cost,
        name="stack",
    )(*pieces)


def polar_kernel(groups, lows, masks, cols_ref, live_ref, virt_ref, occ_ref, *rest):
    rest = list(rest)
    take = lambda n: [rest.pop(0) for _ in range(n)]
    own, others, shares, outs = take(groups), take(lows - 1), take(len(masks)), take(groups)
    dense, lhs, half, full = rest
    slots, width = outs[0].shape[0], outs[0].shape[1]
    basis = virt_ref.shape[0]
    me = lax.axis_index("pair")
    high, low = me // lows, lax.rem(me, lows)

    dense[...] = jnp.zeros_like(dense)
    for e in range(lows):
        for d in range(groups):
            tiles = own[d] if e == 0 else others[e - 1].at[d]
            row = lax.rem(high + groups - d, groups) * lows + lax.rem(low + lows - e, lows)
            for s in range(slots):

                @pl.when(s < live_ref[row])
                def _():
                    dense[rows_at(row, width), rows_at(cols_ref[row, s], width)] = tiles[s]

    lhs[0:width, :] = occ_ref[...]
    for mask_list, share in zip(masks, shares):
        part = width // (len(masks) * len(mask_list))
        for k, mask in enumerate(mask_list):
            source = lax.axis_index("aux") ^ mask if part < width else 0
            for d in range(1, groups):
                base = (groups - d) * width
                for j in range(basis // width):
                    at = j * part
                    lhs[
                        pl.ds(pl.multiple_of(base + source * part, part), part),
                        j * width : (j + 1) * width,
                    ] = share[k, d - 1, at // width, at % width : at % width + part, :]
    wide = 2 * width
    for source, by, into in ((lhs, dense, half), (half, virt_ref, full)):
        for j in range(0, basis, wide):
            into[:, j : j + wide] = jnp.dot(
                source[...], by[:, j : j + wide], preferred_element_type=F32
            ).astype(BF16)
    for d in range(groups):
        row = lax.rem(high + d, groups) * lows + low
        alive = live_ref[row]
        for s in range(slots):
            tile = full[d * width : (d + 1) * width, rows_at(cols_ref[row, s], width)]
            outs[d][s] = jnp.where(s < alive, tile, jnp.zeros_like(tile))


def polar(cols, live, virt, occ, own, others, masks, shares):
    groups, lows = len(own), len(others) + 1
    slots, width = own[0].shape[0], own[0].shape[1]
    basis = virt.shape[0]
    shapes = [jax.ShapeDtypeStruct((slots, width, width), BF16)] * groups
    scratch = [(basis, basis)] + [(groups * width, basis)] * 3
    arrays = [virt, occ, *own, *others, *shares]
    held = size_of(arrays) + size_of(shapes) + sum(2 * a * b for a, b in scratch)
    return pl.pallas_call(
        lambda *refs: polar_kernel(groups, lows, masks, *refs),
        out_shape=shapes,
        in_specs=[SMEM, SMEM] + [VMEM] * len(arrays),
        out_specs=[VMEM] * groups,
        scratch_shapes=[pltpu.VMEM(s, BF16) for s in scratch],
        compiler_params=pltpu.CompilerParams(vmem_limit_bytes=held + 12 * MIB),
        cost_estimate=LONG,
        name="polar",
    )(cols, live, *arrays)


def chi_kernel(groups, lows, chunks, factor, places, keep, *rest):
    count = groups * len(chunks)
    everyone, pieces = rest[: len(places)], rest[len(places) : len(places) + count]
    kept = rest[len(rest) - len(places) :] if keep else ()
    prior, out = rest[len(places) + count : -1 - len(kept)], rest[-1 - len(kept)]
    for ref, copy in zip(everyone, kept):
        copy[...] = ref[...]
    _, rows, width = everyone[0].shape
    unit, local = out.shape[1], out.shape[2]
    high, aux = lax.axis_index("pair") // lows, lax.axis_index("aux")
    step = 16

    def pair(ref, r):
        halves = [ref[..., r + k * step : r + (k + 1) * step, :] for k in range(2)]
        return jnp.concatenate([x.reshape(-1, width) for x in halves], axis=1)

    rights = [
        jnp.concatenate([pair(ref, r) for ref in pieces], axis=0) for r in range(0, rows, 2 * step)
    ]

    def product(ref):
        total = jnp.zeros((ref.shape[0] * step, count * step), F32)
        for right, r in zip(rights, range(0, rows, 2 * step)):
            total += lax.dot_general(
                pair(ref, r), right, (((1,), (1,)), ((), ())), preferred_element_type=F32
            )
        row = lax.broadcasted_iota(jnp.int32, total.shape, 0) % step
        col = lax.broadcasted_iota(jnp.int32, total.shape, 1) % step
        total = jnp.where(row == col, total, 0.0).reshape(-1, step, total.shape[1])
        return jnp.sum(total, axis=1)

    for mask in sorted({m for m, _ in places}):
        mine = sorted((start, n) for n, (m, start) in enumerate(places) if m == mask)
        total = [product(everyone[n]) for _, n in mine]
        total = jnp.concatenate(total, axis=0) if len(total) > 1 else total[0]
        group = lax.broadcasted_iota(jnp.int32, total.shape, 1) // step
        place = lax.broadcasted_iota(jnp.int32, (local, local), 1)
        result = jnp.zeros((local, local), F32)
        for n in range(count):
            c, d = divmod(n, groups)
            q = chunks[c] * groups + lax.rem(high + groups - d, groups)
            value = jnp.sum(jnp.where(group == n, total, 0.0), axis=1, keepdims=True)
            result = jnp.where(place == q, value * factor, result)
        for u in range(local // unit):
            at = (aux ^ mask) * (local // unit) + u
            piece = result[u * unit : (u + 1) * unit]
            out[at] = piece + prior[0][at] if prior else piece


def chi(everyone, back, chunks, prior, groups, lows, local, unit, factor, keep=False):
    pieces = [p for c in chunks for p in back[c]]
    slots, width = pieces[0].shape[0], pieces[0].shape[1]
    places = [place for place, _ in everyone]
    arrays = [e.reshape(-1, slots * width, width) for _, e in everyone]
    arrays += [p.reshape(slots * width, width) for p in pieces]
    if prior is not None:
        arrays.append(prior)
    count = sum(e.shape[0] for _, e in everyone)
    part, *kept = pl.pallas_call(
        lambda *refs: chi_kernel(groups, lows, chunks, factor, places, keep, *refs),
        out_shape=[jax.ShapeDtypeStruct((count // unit, unit, local), F32)]
        + [pltpu.VMEM(a.shape, a.dtype) for a in arrays[: len(places)] if keep],
        in_specs=[VMEM] * len(arrays),
        out_specs=[VMEM] * (1 + len(places) * keep),
        compiler_params=pltpu.CompilerParams(vmem_limit_bytes=size_of(arrays) + 12 * MIB),
        cost_estimate=MIDDLE,
        name="chi",
    )(*arrays)
    return part, [(place, e) for place, e in zip(places, kept)] if keep else everyone


def per_device(three_centre, occ_green, virt_green, tile_cols, tile_live):
    local, slots, width, _ = three_centre.shape
    blocks, peers = lax.axis_size("pair"), lax.axis_size("aux")
    groups = math.gcd(local, blocks)
    lows = blocks // groups
    chunks = local // groups
    shares = peers if peers & (peers - 1) == 0 and blocks % peers == 0 else 1

    def along_high(array, d):
        moves = [
            (h * lows + l, (h + d) % groups * lows + l) for h in range(groups) for l in range(lows)
        ]
        return lax.ppermute(array, "pair", moves)

    def along_low(array, e):
        moves = [
            (h * lows + l, h * lows + (l + e) % lows) for h in range(groups) for l in range(lows)
        ]
        return lax.ppermute(array, "pair", moves)

    def swap(array, bit):
        return lax.ppermute(array, "aux", [(a, a ^ bit) for a in range(peers)])

    def shift(arrays, between=lambda: None):
        order = sorted(range(1, groups), key=lambda d: (min(d, groups - d), -d))
        moved = {0: arrays[0]}
        for d in order:
            moved[d] = along_high(arrays[d], d)
            if d == order[-1]:
                between()
        return [moved[d] for d in range(groups)]

    together = lax.optimization_barrier
    factor = 1.0 / (width * math.sqrt(slots * blocks))
    bits = [1 << n for n in reversed(range(peers.bit_length() - 1))]
    own, others, tiles, back = {}, {}, {}, {}
    parts, masks = [], [[0]]
    everyone = [((0, 0), three_centre)]
    part, per = None, local * peers // blocks
    unit = math.gcd(local, per)

    first_back = max(chunks, 3)
    cut = -(-local * 7 // 12) if chunks > 1 else local
    first, copies = split(three_centre, occ_green, groups, lows, 0, shares)
    sending = {0: first}
    for phase in range(first_back + chunks):

        def share_low():
            if phase - 1 in own:
                stacked, *extra = stack(own[phase - 1], slots, QUICK if phase == chunks else LONG)
                if extra:
                    parts[:] = [extra[0][None]]
                others[phase - 1] = [along_low(stacked, e) for e in range(1, lows)]

        if phase in sending:
            own[phase] = shift(sending.pop(phase), share_low)
        elif phase >= first_back:
            back[phase - first_back] = shift(tiles.pop(phase - first_back), share_low)
        else:
            share_low()
        if phase in (1, 2):
            for bit in bits[: len(bits) - 1] if phase == 1 else bits[len(bits) - 1 :]:
                parts, masks = parts + [swap(x, bit) for x in parts], masks + [[m[0] | bit] for m in masks]
        for c in range(1, chunks):
            if phase == c - 1:
                runs = ([(0, cut)] * (c == 1) + [(cut, local)] * (c == chunks - 1)) * (cut < local)
                sending[c], more = split(three_centre, occ_green, groups, lows, c, shares, runs)
                copies = copies + more
        if phase == 0 and bits:
            first_part = swap(copies[0] if copies else three_centre, bits[0])
            everyone.append(((bits[0], 0), first_part))
            if len(bits) > 1:
                everyone.append(((bits[-1], 0), swap(three_centre, bits[-1])))
        if phase == first_back - 1 and bits and cut < local:
            everyone.append(((bits[0], cut), swap(copies[1], bits[0])))
        if phase - 2 in others:
            c, pieces = phase - 2, own[phase - 2]
            if phase == first_back - 1 + 1 and everyone[-1][0][1]:
                pieces = together((pieces, everyone[-1][1]))[0]
            tiles[c] = list(
                polar(tile_cols, tile_live, virt_green, occ_green, pieces, others.pop(c), masks, parts)
            )
        if phase == first_back + chunks - 1:
            for bit in bits[1:]:
                for (mask, start), array in list(everyone):
                    if (mask ^ bit, start) not in dict(everyone):
                        array = together((array, back[chunks - 2]))[0]
                        everyone.append(((mask ^ bit, start), swap(array, bit)))
            if chunks > 1:
                part, everyone = chi(
                    everyone, back, list(range(chunks - 1)), None, groups, lows, local, unit, factor, True
                )
        done = {}
        if phase == 0 and len(bits) > 1:
            done[2] = everyone[2][1]
        if phase == 1 and bits:
            done[1] = everyone[1][1]
        live = (three_centre, sending, copies, own if phase < first_back else {}, tiles, back, parts, part, done)
        three_centre, sending, copies, kept, tiles, back, parts, part, done = together(live)
        own = kept or own
        for n, array in done.items():
            everyone[n] = (everyone[n][0], array)
    part, _ = chi(everyone, back, [chunks - 1], part, groups, lows, local, unit, factor)
    part = part.reshape(blocks, per, local)
    return jnp.sum(lax.all_to_all(part, "pair", 0, 0, tiled=True), axis=0)


def solution(mesh):
    placed = (P("aux", "pair", None, None), P("pair", None), P(), P(), P())
    return jax.shard_map(
        per_device, mesh=mesh, in_specs=placed, out_specs=P("pair", "aux"), check_vma=False
    )
```
